256 devices in a mesh: row: 16 (over z, core), col: 16 (over x, y).
Axes of the slice: x: 4, y: 4, z: 8, core: 2. Of those that a mesh axis runs over, the one named last changes fastest.
Arguments:
- tokens: bfloat16 [2048, 12288], P('row', 'col'), may hold values from -6 to 6
- weight: bfloat16 [12288, 24576], P('col', 'row'), may hold values from -0.0546875 to 0.0546875
- cotangent: bfloat16 [2048, 24576], P('col', 'row'), may hold values from -6 to 6
Outputs:
- hidden: bfloat16 [2048, 24576], P('col', 'row')
- grad_weight: float32 [12288, 24576], P('col', 'row')
- grad_tokens: bfloat16 [2048, 12288], P('row', 'col')
The draws below stay inside these ranges and needn't reach their ends.
All inputs are finite; a program needn't handle non-finite values.
Results may differ from the reference program's by a relative error of at most 0.0049.
Values may be sent and summed in bfloat16 or wider, within the bound.
No kernel may reach another device: no remote copies, remote signals or barrier semaphores. Data moves between devices by JAX's collectives and lax.ppermute only.
A program may use at most 128 MiB of HBM per device.

```python
import math
import jax
import jax.numpy as jnp
from jax import lax

D = 12288
F = 24576
TOKENS = 2048


def steps_of(rng, dims, cuts, least, high):
    level, own = 1.0, jax.random.fold_in(rng, 6)
    for dim, blocks in cuts:
        steps = jnp.exp(jax.random.uniform(jax.random.fold_in(own, dim), (blocks,), jnp.float32, least / len(cuts), high / len(cuts)))
        level = level * jnp.repeat(steps, dims[dim] // blocks).reshape([-1 if axis == dim else 1 for axis in range(len(dims))])
    return level


def scatter_about(own_key, shape, deviation, bound, pieces=(), dtype=jnp.bfloat16):
    result = deviation * jax.random.normal(own_key, shape, jnp.float32)
    if pieces:
        result = result * steps_of(own_key, shape, pieces, -0.22, 0.18)
    return jnp.clip(result, -bound, bound).astype(dtype)


def setup_inputs(seed: int = 0) -> dict:
    seeds = jax.random.split(jax.random.key(seed), 4)
    return {
        "tokens": scatter_about(seeds[0], (TOKENS, D), 1.0, 6.0, ((0, 16), (1, 16))),
        "weight": scatter_about(seeds[1], (D, F), D ** -0.5, 0.0546875, ((0, 16), (1, 16))),
        "cotangent": scatter_about(seeds[2], (TOKENS, F), 1.0, 6.0, ((0, 16), (1, 16))),
    }


def gelu_exact(value):
    return 0.5 * value * (1.0 + jax.scipy.special.erf(value / math.sqrt(2.0)))

def gelu_slope(value):
    cumulative = 0.5 * (1.0 + jax.scipy.special.erf(value / math.sqrt(2.0)))
    return cumulative + value * jnp.exp(-0.5 * value * value) / math.sqrt(2.0 * math.pi)

def reference(tokens, weight, cotangent):
    pre = jnp.dot(tokens, weight, preferred_element_type=jnp.float32)
    hidden = gelu_exact(pre).astype(jnp.bfloat16)
    grad_pre = (cotangent.astype(jnp.float32) * gelu_slope(pre)).astype(jnp.bfloat16)
    grad_weight = lax.dot_general(tokens, grad_pre, (((0,), (0,)), ((), ())), preferred_element_type=jnp.float32)
    grad_tokens = lax.dot_general(grad_pre, weight, (((1,), (1,)), ((), ())), preferred_element_type=jnp.float32)
    return (hidden, grad_weight, grad_tokens.astype(jnp.bfloat16))
```

```python
import math

import jax
import jax.numpy as jnp
from jax import lax
from jax.sharding import PartitionSpec as P

F32, BF16 = jnp.float32, jnp.bfloat16
CHUNKS = 2


def gelu_and_slope(value):
    cumulative = 0.5 * (1.0 + jax.scipy.special.erf(value / math.sqrt(2.0)))
    density = jnp.exp(-0.5 * value * value) / math.sqrt(2.0 * math.pi)
    return value * cumulative, cumulative + value * density


def dot(a, b):
    return lax.dot_general(a, b, (((a.ndim - 1,), (0,)), ((), ())), preferred_element_type=F32)


def dot_t(a, b):
    return lax.dot_general(a, b, (((a.ndim - 1,), (1,)), ((), ())), preferred_element_type=F32)


def shift_x(k):
    return [(x * 4 + y, (x + k) % 4 * 4 + y) for x in range(4) for y in range(4)]


def shift_y(k):
    return [(x * 4 + y, x * 4 + (y + k) % 4) for x in range(4) for y in range(4)]


def shift_z(k):
    return [(z * 2 + c, (z + k) % 8 * 2 + c) for z in range(8) for c in range(2)]


SWAP = [(z * 2 + c, z * 2 + 1 - c) for z in range(8) for c in range(2)]


def cat(*parts):
    return jnp.concatenate(parts, axis=0)


def from_relative(blocks, me):
    n = len(blocks)
    twice = jnp.stack(blocks + blocks[:-1])
    return lax.dynamic_slice_in_dim(twice, (n - me) % n, n, axis=0)


def pick(array, index):
    return lax.dynamic_index_in_dim(array, index, axis=0, keepdims=False)


def gather_z(block, z):
    half = block.shape[0] // 2
    up, down = [block], [block]
    for _ in range(3):
        up.append(lax.ppermute(up[-1], "row", shift_z(1)))
        down.append(lax.ppermute(down[-1], "row", shift_z(-1)))
    far = cat(
        lax.ppermute(up[3][:half], "row", shift_z(1)),
        lax.ppermute(down[3][half:], "row", shift_z(-1)),
    )
    return from_relative([block, down[1], down[2], down[3], far, up[3], up[2], up[1]], z)


def reduce4(part, half, shift):
    low, high, every = slice(0, half), slice(half, 2 * half), slice(0, 2 * half)
    left = cat(part(2, low), part(3, high)).astype(BF16)
    right = cat(part(1, low), part(2, high)).astype(BF16)
    from_right = lax.ppermute(left, "col", shift(-1))
    from_left = lax.ppermute(right, "col", shift(1))
    left = (part(3, low) + from_right[low].astype(F32)).astype(BF16)
    right = (part(1, high) + from_left[high].astype(F32)).astype(BF16)
    last_right = lax.ppermute(left, "col", shift(-1))
    last_left = lax.ppermute(right, "col", shift(1))
    first = cat(from_left[low], from_right[high]).astype(F32)
    return part(0, every) + first + cat(last_right, last_left).astype(F32)


def gather4(block, half, shift):
    from_right = lax.ppermute(block, "col", shift(-1))
    from_left = lax.ppermute(block, "col", shift(1))
    far = cat(
        lax.ppermute(from_right[:half], "col", shift(-1)),
        lax.ppermute(from_left[half:], "col", shift(1)),
    )
    return [block, from_right, far, from_left]


def shards(tokens, weight, cotangent):
    row, col = lax.axis_index("row"), lax.axis_index("col")
    z, core = row // 2, row % 2
    x, y = col // 4, col % 4
    rows = tokens.shape[0] // CHUNKS
    width, hidden_width = weight.shape

    gathered = []
    for u in range(CHUNKS):
        mine = gather_z(tokens[u * rows : (u + 1) * rows], z)
        other = lax.ppermute(mine, "row", SWAP)
        zero, one = jnp.where(core == 0, mine, other), jnp.where(core == 0, other, mine)
        full = jnp.stack([zero, one], axis=1).reshape(4, 4, rows, width)
        gathered.append(full if u % 2 == 0 else full.swapaxes(0, 1))

    hiddens, grads = [], []
    for u in range(CHUNKS):
        full = gathered[u]
        (a, shift_a), (b, shift_b) = ((x, shift_x), (y, shift_y))[:: 1 if u % 2 == 0 else -1]
        near = [pick(full, (a + k) % 4) for k in range(4)]
        near = [n.reshape(4 * rows, width) for n in near]
        summed = reduce4(lambda k, s: dot(near[k][s], weight), 2 * rows, shift_a)
        summed = summed.reshape(4, rows, hidden_width)
        terms = [pick(summed, (b + k) % 4) for k in range(4)]
        pre = reduce4(lambda k, s: terms[k][s], rows // 2, shift_b)
        value, slope = gelu_and_slope(pre)
        hiddens.append(value.astype(BF16))
        grad = (cotangent[u * rows : (u + 1) * rows].astype(F32) * slope).astype(BF16)
        block = from_relative(gather4(grad, rows // 2, shift_b), b)
        block = gather4(block.reshape(4 * rows, hidden_width), 2 * rows, shift_a)
        grads.append(from_relative(block, a).reshape(4, 4, rows, hidden_width))

    outs, grad_weight = [], None
    for u in range(CHUNKS):
        grad = grads[u]
        if u % 2 == 0:
            parity = grad.reshape(8, 2, rows, hidden_width)
            mine, other = (lax.dynamic_index_in_dim(parity, c, 1, False) for c in (core, 1 - core))
            place = lambda p: p
        else:
            parity = grad.reshape(2, 2, 4, rows, hidden_width)
            mine, other = (lax.dynamic_index_in_dim(parity, c, 1, False) for c in (core, 1 - core))
            place = lambda p: p % 2 * 4 + p // 2
        away = dot_t(other.reshape(8 * rows, hidden_width), weight).astype(BF16)
        away = lax.ppermute(away, "row", SWAP)
        part = dot_t(mine.reshape(8 * rows, hidden_width), weight) + away.astype(F32)
        part = part.reshape(8, rows, width)
        total = pick(part, place(z))
        for k in (4, 3, 5, 2, 6, 1, 7):
            term = pick(part, place((z + k) % 8)).astype(BF16)
            total += lax.ppermute(term, "row", shift_z(k)).astype(F32)
        outs.append(total.astype(BF16))
        term = lax.dot_general(
            gathered[u].reshape(-1, width),
            grad.reshape(-1, hidden_width),
            (((0,), (0,)), ((), ())),
            preferred_element_type=F32,
        )
        grad_weight = term if grad_weight is None else grad_weight + term
    return cat(*hiddens), grad_weight, cat(*outs)


def solution(mesh):
    in_specs = (P("row", "col"), P("col", "row"), P("col", "row"))
    out_specs = (P("col", "row"), P("col", "row"), P("row", "col"))
    return jax.shard_map(shards, mesh=mesh, in_specs=in_specs, out_specs=out_specs, check_vma=False)
```

```python
import math

import jax
import jax.numpy as jnp
from jax import lax
from jax.experimental import pallas as pl
from jax.experimental.pallas import tpu as pltpu
from jax.sharding import PartitionSpec as P

F32, BF16 = jnp.float32, jnp.bfloat16
CHUNKS = 2


def gelu_and_slope(value):
    cumulative = 0.5 * (1.0 + jax.scipy.special.erf(value / math.sqrt(2.0)))
    density = jnp.exp(-0.5 * value * value) / math.sqrt(2.0 * math.pi)
    return value * cumulative, cumulative + value * density


def dot(a, b):
    return lax.dot_general(a, b, (((a.ndim - 1,), (0,)), ((), ())), preferred_element_type=F32)


def dot_t(a, b):
    return lax.dot_general(a, b, (((a.ndim - 1,), (1,)), ((), ())), preferred_element_type=F32)


def shift_x(k):
    return [(x * 4 + y, (x + k) % 4 * 4 + y) for x in range(4) for y in range(4)]


def shift_y(k):
    return [(x * 4 + y, x * 4 + (y + k) % 4) for x in range(4) for y in range(4)]


def shift_z(k):
    return [(z * 2 + c, (z + k) % 8 * 2 + c) for z in range(8) for c in range(2)]


SWAP = [(z * 2 + c, z * 2 + 1 - c) for z in range(8) for c in range(2)]


def cat(*parts):
    return jnp.concatenate(parts, axis=0)


def from_relative(blocks, me):
    n = len(blocks)
    twice = jnp.stack(blocks + blocks[:-1])
    return lax.dynamic_slice_in_dim(twice, (n - me) % n, n, axis=0)


def pick(array, index):
    return lax.dynamic_index_in_dim(array, index, axis=0, keepdims=False)


def place_kernel(count, *refs):
    blocks, first, second, sems = refs[:count], refs[count], refs[count + 1], refs[count + 2]
    row = lax.axis_index("row")
    z, core = row // 2, row % 2
    half = first.shape[2]
    copies = []

    def put(source, start, k, parity, part):
        there = (z + k) % 8
        x, y = there // 2, there % 2 * 2 + parity
        target = first.at[x, y] if part == 0 else second.at[y, x]
        copy = pltpu.make_async_copy(source.at[pl.ds(start, half)], target, sems.at[len(copies)])
        copy.start()
        copies.append(copy)

    distances = [[0], [7], [1], [6], [2], [5], [3], [0, 7, 1], [6, 2, 5, 3], [4], [4]]
    parities = [core] * 7 + [1 - core, 1 - core, core, 1 - core]
    for source, ks, parity in zip(blocks, distances, parities):
        for i, k in enumerate(ks):
            for part in range(2):
                put(source, (2 * i + part) * half, k, parity, part)
    for copy in copies:
        copy.wait()


def gather_tokens(block):
    half, width = block.shape[0] // 2, block.shape[1]
    up, down = [block], [block]
    for _ in range(3):
        up.append(lax.ppermute(up[-1], "row", shift_z(1)))
        down.append(lax.ppermute(down[-1], "row", shift_z(-1)))
    far = cat(
        lax.ppermute(up[3][:half], "row", shift_z(1)),
        lax.ppermute(down[3][half:], "row", shift_z(-1)),
    )
    near = lax.ppermute(cat(block, up[1], down[1]), "row", SWAP)
    middle = lax.ppermute(cat(up[2], down[2], up[3], down[3]), "row", SWAP)
    last = lax.ppermute(far, "row", SWAP)
    blocks = [block, up[1], down[1], up[2], down[2], up[3], down[3], near, middle, far, last]
    shape = jax.ShapeDtypeStruct((4, 4, half, width), block.dtype)
    return pl.pallas_call(
        lambda *refs: place_kernel(len(blocks), *refs),
        out_shape=(shape, shape),
        in_specs=[pl.BlockSpec(memory_space=pl.ANY)] * len(blocks),
        out_specs=(pl.BlockSpec(memory_space=pl.ANY),) * 2,
        scratch_shapes=[pltpu.SemaphoreType.DMA((32,))],
        cost_estimate=pl.CostEstimate(flops=0, bytes_accessed=8 * half * width * 32, transcendentals=0),
        name="place_tokens",
    )(*blocks)


def reduce4(part, half, shift):
    low, high, every = slice(0, half), slice(half, 2 * half), slice(0, 2 * half)
    left = cat(part(2, low), part(3, high)).astype(BF16)
    right = cat(part(1, low), part(2, high)).astype(BF16)
    from_right = lax.ppermute(left, "col", shift(-1))
    from_left = lax.ppermute(right, "col", shift(1))
    left = (part(3, low) + from_right[low].astype(F32)).astype(BF16)
    right = (part(1, high) + from_left[high].astype(F32)).astype(BF16)
    last_right = lax.ppermute(left, "col", shift(-1))
    last_left = lax.ppermute(right, "col", shift(1))
    first = cat(from_left[low], from_right[high]).astype(F32)
    return part(0, every) + first + cat(last_right, last_left).astype(F32)


def gather4(block, half, shift):
    from_right = lax.ppermute(block, "col", shift(-1))
    from_left = lax.ppermute(block, "col", shift(1))
    far = cat(
        lax.ppermute(from_right[:half], "col", shift(-1)),
        lax.ppermute(from_left[half:], "col", shift(1)),
    )
    return [block, from_right, far, from_left]


def shards(tokens, weight, cotangent):
    row, col = lax.axis_index("row"), lax.axis_index("col")
    z, core = row // 2, row % 2
    x, y = col // 4, col % 4
    rows = tokens.shape[0] // CHUNKS
    width, hidden_width = weight.shape

    gathered = gather_tokens(tokens)
    hiddens, grads = [], []
    for u in range(CHUNKS):
        full = gathered[u]
        (a, shift_a), (b, shift_b) = ((x, shift_x), (y, shift_y))[:: 1 if u % 2 == 0 else -1]
        near = [pick(full, (a + k) % 4) for k in range(4)]
        near = [n.reshape(4 * rows, width) for n in near]
        summed = reduce4(lambda k, s: dot(near[k][s], weight), 2 * rows, shift_a)
        summed = summed.reshape(4, rows, hidden_width)
        terms = [pick(summed, (b + k) % 4) for k in range(4)]
        pre = reduce4(lambda k, s: terms[k][s], rows // 2, shift_b)
        value, slope = gelu_and_slope(pre)
        hiddens.append(value.astype(BF16))
        grad = (cotangent[u * rows : (u + 1) * rows].astype(F32) * slope).astype(BF16)
        block = from_relative(gather4(grad, rows // 2, shift_b), b)
        block = gather4(block.reshape(4 * rows, hidden_width), 2 * rows, shift_a)
        grads.append(from_relative(block, a).reshape(4, 4, rows, hidden_width))

    terms, grad_weight = [], None
    for u in range(CHUNKS):
        if u % 2 == 0:
            parity = grads[u].reshape(8, 2, rows, hidden_width)
        else:
            parity = grads[u].reshape(2, 2, 4, rows, hidden_width)
        mine, other = (
            lax.dynamic_index_in_dim(parity, c, 1, False).reshape(8 * rows, hidden_width)
            for c in (core, 1 - core)
        )
        away = lax.ppermute(dot_t(other, weight).astype(BF16), "row", SWAP)
        terms.append((dot_t(mine, weight) + away.astype(F32)).reshape(8, rows, width))

    def term(k):
        there = (z + k) % 8
        return pick(terms[0], there), pick(terms[1], there % 2 * 4 + there // 2)

    left = lax.ppermute(term(4)[0].astype(BF16), "row", shift_z(-1))
    right = lax.ppermute(term(4)[1].astype(BF16), "row", shift_z(1))
    for step in range(3):
        first, second = term(5 + step)
        if step == 0:
            left = cat((first + left.astype(F32)).astype(BF16), second.astype(BF16))
        else:
            left = (cat(first, second) + left.astype(F32)).astype(BF16)
        first, second = term(3 - step)
        if step == 0:
            right = cat(first.astype(BF16), (second + right.astype(F32)).astype(BF16))
        else:
            right = (cat(first, second) + right.astype(F32)).astype(BF16)
        left = lax.ppermute(left, "row", shift_z(-1))
        right = lax.ppermute(right, "row", shift_z(1))
    grad_tokens = cat(*term(0)) + left.astype(F32) + right.astype(F32)
    for u in range(CHUNKS):
        product = lax.dot_general(
            gathered[u].reshape(-1, width),
            grads[u].reshape(-1, hidden_width),
            (((0,), (0,)), ((), ())),
            preferred_element_type=F32,
        )
        grad_weight = product if grad_weight is None else grad_weight + product
    return cat(*hiddens), grad_weight, grad_tokens.astype(BF16)


def solution(mesh):
    in_specs = (P("row", "col"), P("col", "row"), P("col", "row"))
    out_specs = (P("col", "row"), P("col", "row"), P("row", "col"))
    return jax.shard_map(shards, mesh=mesh, in_specs=in_specs, out_specs=out_specs, check_vma=False)
```

```python
import math

import jax
import jax.numpy as jnp
from jax import lax
from jax.experimental import pallas as pl
from jax.experimental.pallas import tpu as pltpu
from jax.sharding import PartitionSpec as P

F32, BF16 = jnp.float32, jnp.bfloat16
CHUNKS = 2


def gelu_and_slope(value):
    cumulative = 0.5 * (1.0 + jax.scipy.special.erf(value / math.sqrt(2.0)))
    density = jnp.exp(-0.5 * value * value) / math.sqrt(2.0 * math.pi)
    return value * cumulative, cumulative + value * density


def dot(a, b):
    return lax.dot_general(a, b, (((a.ndim - 1,), (0,)), ((), ())), preferred_element_type=F32)


def dot_t(a, b):
    return lax.dot_general(a, b, (((a.ndim - 1,), (1,)), ((), ())), preferred_element_type=F32)


def shift_x(k):
    return [(x * 4 + y, (x + k) % 4 * 4 + y) for x in range(4) for y in range(4)]


def shift_y(k):
    return [(x * 4 + y, x * 4 + (y + k) % 4) for x in range(4) for y in range(4)]


def shift_z(k):
    return [(z * 2 + c, (z + k) % 8 * 2 + c) for z in range(8) for c in range(2)]


SWAP = [(z * 2 + c, z * 2 + 1 - c) for z in range(8) for c in range(2)]


def cat(*parts):
    return jnp.concatenate(parts, axis=0)


def from_relative(blocks, me):
    n = len(blocks)
    twice = jnp.stack(blocks + blocks[:-1])
    return lax.dynamic_slice_in_dim(twice, (n - me) % n, n, axis=0)


def pick(array, index):
    return lax.dynamic_index_in_dim(array, index, axis=0, keepdims=False)


def place_kernel(count, *refs):
    blocks, first, second = refs[:count], refs[count], refs[count + 1]
    row = lax.axis_index("row")
    z, core = row // 2, row % 2
    half = first.shape[2]
    distances = [[0], [7], [1], [6], [2], [5], [3], [0, 7, 1], [6, 2], [5, 3], [4], [4]]
    parities = [core] * 7 + [1 - core] * 3 + [core, 1 - core]
    for source, ks, parity in zip(blocks, distances, parities):
        for i, k in enumerate(ks):
            there = (z + k) % 8
            x, y = there // 2, there % 2 * 2 + parity
            first[x, y] = source[pl.ds(2 * i * half, half), :]
            second[y, x] = source[pl.ds((2 * i + 1) * half, half), :]


def after(value, *others):
    return lax.optimization_barrier((value, *others))[0]


def gather_tokens(block):
    half, width = block.shape[0] // 2, block.shape[1]
    swap = lambda *parts: lax.ppermute(cat(*parts), "row", SWAP)
    above = lambda part: lax.ppermute(part, "row", shift_z(1))
    below = lambda part: lax.ppermute(part, "row", shift_z(-1))
    up1, down1 = above(block), below(block)
    up2, down2 = above(up1), below(down1)
    near = swap(block, up1, down1)
    up3, down3 = above(after(up2, near)), below(after(down2, near))
    middle = swap(up2, down2)
    far = cat(above(after(up3, middle)[:half]), below(after(down3, middle)[half:]))
    outer = swap(up3, down3)
    last = swap(far)
    blocks = [block, up1, down1, up2, down2, up3, down3, near, middle, outer, far, last]
    shape = jax.ShapeDtypeStruct((4, 4, half, width), block.dtype)
    return pl.pallas_call(
        lambda *refs: place_kernel(len(blocks), *refs),
        out_shape=(shape, shape),
        in_specs=[pl.BlockSpec(memory_space=pltpu.VMEM)] * len(blocks),
        out_specs=(pl.BlockSpec(memory_space=pltpu.VMEM),) * 2,
        compiler_params=pltpu.CompilerParams(vmem_limit_bytes=16 * 2**20),
        cost_estimate=pl.CostEstimate(flops=0, bytes_accessed=128 * half * width, transcendentals=0),
        name="place_tokens",
    )(*blocks)


def reduce4(part, half, shift, split):
    low, high, every = slice(0, half), slice(half, 2 * half), slice(0, 2 * half)
    leftward = lambda *parts: lax.ppermute(cat(*parts).astype(BF16), "col", shift(-1))
    rightward = lambda *parts: lax.ppermute(cat(*parts).astype(BF16), "col", shift(1))
    if split:
        relay_left, relay_right = leftward(part(2, low)), rightward(part(2, high))
        near_high, near_low = leftward(part(3, high)), rightward(part(1, low))
    else:
        from_right = leftward(part(2, low), part(3, high))
        from_left = rightward(part(1, low), part(2, high))
        relay_left, near_high = from_right[low], from_right[high]
        near_low, relay_right = from_left[low], from_left[high]
    last_low = leftward(part(3, low) + relay_left.astype(F32))
    last_high = rightward(part(1, high) + relay_right.astype(F32))
    return part(0, every) + cat(near_low, near_high).astype(F32) + cat(last_low, last_high).astype(F32)


def gather4(block, half, shift, split):
    leftward = lambda part: lax.ppermute(part, "col", shift(-1))
    rightward = lambda part: lax.ppermute(part, "col", shift(1))
    if split:
        low, high = leftward(block[:half]), rightward(block[half:])
        from_right = cat(low, leftward(block[half:]))
        from_left = cat(rightward(block[:half]), high)
    else:
        from_right, from_left = leftward(block), rightward(block)
        low, high = from_right[:half], from_left[half:]
    return [block, from_right, cat(leftward(low), rightward(high)), from_left]


def shards(tokens, weight, cotangent):
    row, col = lax.axis_index("row"), lax.axis_index("col")
    z, core = row // 2, row % 2
    x, y = col // 4, col % 4
    rows = tokens.shape[0] // CHUNKS
    width, hidden_width = weight.shape

    gathered = gather_tokens(tokens)
    hiddens, grads = [], []
    for u in range(CHUNKS):
        full = gathered[u]
        (a, shift_a), (b, shift_b) = ((x, shift_x), (y, shift_y))[:: 1 if u % 2 == 0 else -1]
        near = [pick(full, (a + k) % 4) for k in range(4)]
        near = [n.reshape(4 * rows, width) for n in near]
        summed = reduce4(lambda k, s: dot(near[k][s], weight), 2 * rows, shift_a, True)
        summed = summed.reshape(4, rows, hidden_width)
        terms = [pick(summed, (b + k) % 4) for k in range(4)]
        pre = reduce4(lambda k, s: terms[k][s], rows // 2, shift_b, False)
        value, slope = gelu_and_slope(pre)
        hiddens.append(value.astype(BF16))
        grad = (cotangent[u * rows : (u + 1) * rows].astype(F32) * slope).astype(BF16)
        block = from_relative(gather4(grad, rows // 2, shift_b, False), b)
        block = gather4(block.reshape(4 * rows, hidden_width), 2 * rows, shift_a, True)
        grads.append(from_relative(block, a).reshape(4, 4, rows, hidden_width))

    terms, grad_weight = [], None
    for u in range(CHUNKS):
        if u % 2 == 0:
            parity = grads[u].reshape(8, 2, rows, hidden_width)
        else:
            parity = grads[u].reshape(2, 2, 4, rows, hidden_width)
        mine, other = (
            lax.dynamic_index_in_dim(parity, c, 1, False).reshape(8 * rows, hidden_width)
            for c in (core, 1 - core)
        )
        away = lax.ppermute(dot_t(other, weight).astype(BF16), "row", SWAP)
        terms.append((dot_t(mine, weight) + away.astype(F32)).reshape(8, rows, width))

    def term(k):
        there = (z + k) % 8
        return pick(terms[0], there), pick(terms[1], there % 2 * 4 + there // 2)

    left = lax.ppermute(term(4)[0].astype(BF16), "row", shift_z(-1))
    right = lax.ppermute(term(4)[1].astype(BF16), "row", shift_z(1))
    for step in range(3):
        first, second = term(5 + step)
        if step == 0:
            left = cat((first + left.astype(F32)).astype(BF16), second.astype(BF16))
        else:
            left = (cat(first, second) + left.astype(F32)).astype(BF16)
        first, second = term(3 - step)
        if step == 0:
            right = cat(first.astype(BF16), (second + right.astype(F32)).astype(BF16))
        else:
            right = (cat(first, second) + right.astype(F32)).astype(BF16)
        left = lax.ppermute(left, "row", shift_z(-1))
        right = lax.ppermute(right, "row", shift_z(1))
    grad_tokens = cat(*term(0)) + left.astype(F32) + right.astype(F32)
    for u in range(CHUNKS):
        product = lax.dot_general(
            gathered[u].reshape(-1, width),
            grads[u].reshape(-1, hidden_width),
            (((0,), (0,)), ((), ())),
            preferred_element_type=F32,
        )
        grad_weight = product if grad_weight is None else grad_weight + product
    return cat(*hiddens), grad_weight, grad_tokens.astype(BF16)


def solution(mesh):
    in_specs = (P("row", "col"), P("col", "row"), P("col", "row"))
    out_specs = (P("col", "row"), P("col", "row"), P("row", "col"))
    return jax.shard_map(shards, mesh=mesh, in_specs=in_specs, out_specs=out_specs, check_vma=False)
```

```python
import math

import jax
import jax.numpy as jnp
from jax import lax
from jax.experimental import pallas as pl
from jax.experimental.pallas import tpu as pltpu
from jax.sharding import PartitionSpec as P

F32, BF16 = jnp.float32, jnp.bfloat16


def gelu_and_slope(value):
    cumulative = 0.5 * (1.0 + jax.scipy.special.erf(value / math.sqrt(2.0)))
    density = jnp.exp(-0.5 * value * value) / math.sqrt(2.0 * math.pi)
    return value * cumulative, cumulative + value * density


def dot(a, b):
    return lax.dot_general(a, b, (((1,), (0,)), ((), ())), preferred_element_type=F32)


def dot_t(a, b):
    return lax.dot_general(a, b, (((1,), (1,)), ((), ())), preferred_element_type=F32)


def shift_plane(k, first):
    pairs = []
    for row in range(16):
        along_x = (row % 2 == 0) == first
        for x in range(4):
            for y in range(4):
                to = (x + k) % 4 * 4 + y if along_x else x * 4 + (y + k) % 4
                pairs.append((row * 16 + x * 4 + y, row * 16 + to))
    return pairs


def shift_z(k):
    return [(z * 2 + c, (z + k) % 8 * 2 + c) for z in range(8) for c in range(2)]


SWAP = [(z * 2 + c, z * 2 + 1 - c) for z in range(8) for c in range(2)]


def cat(*parts):
    return jnp.concatenate(parts, axis=0)


def pick(array, index):
    return lax.dynamic_index_in_dim(array, index, axis=0, keepdims=False)


def copy_call(kernel, out_shapes, *arrays):
    shapes = [jax.ShapeDtypeStruct(shape, BF16) for shape in out_shapes]
    size = 2 * sum(math.prod(s) for s in out_shapes) + 2 * sum(a.size for a in arrays)
    return pl.pallas_call(
        lambda *refs: kernel(refs[: len(arrays)], *refs[len(arrays) :]),
        out_shape=shapes,
        in_specs=[pl.BlockSpec(memory_space=pltpu.VMEM)] * len(arrays),
        out_specs=[pl.BlockSpec(memory_space=pltpu.VMEM)] * len(shapes),
        compiler_params=pltpu.CompilerParams(vmem_limit_bytes=32 * 2**20),
        cost_estimate=pl.CostEstimate(flops=0, bytes_accessed=size, transcendentals=0),
    )(*arrays)


def place_tokens(blocks, tiles, pairs):
    row = lax.axis_index("row")
    z, core = row // 2, row % 2
    rows = tiles.shape[2]
    distances = [[0], [7], [1], [6], [2], [5], [3], None, None, [0, 7, 1, 6, 2], [5, 3, 4]]

    def put(value, k, other, part):
        there = (z + k) % 8
        x, y = there // 2, there % 2 * 2 + (1 - core if other else core)
        first, second = x + core * (y - x), y + core * (x - y)
        tiles[first, second, part, :] = value
        pairs[int(other), there, part, :] = value

    half = rows // 2
    put(blocks[7][...], 4, False, slice(0, half))
    put(blocks[8][...], 4, False, slice(half, rows))
    for n, ks in enumerate(distances):
        for i, k in enumerate(ks or ()):
            put(blocks[n][pl.ds(i * rows, rows), :], k, n >= 9, slice(0, rows))


def gather_tokens(block):
    rows, width = block.shape
    swap = lambda *parts: lax.ppermute(cat(*parts), "row", SWAP)
    above = lambda part: lax.ppermute(part, "row", shift_z(1))
    below = lambda part: lax.ppermute(part, "row", shift_z(-1))
    up1, down1 = above(block), below(block)
    up2, down2 = above(up1), below(down1)
    up3, down3 = above(up2), below(down2)
    near = swap(block, up1, down1, up2, down2)
    far_low, far_high = above(up3[: rows // 2]), below(down3[rows // 2 :])
    outer = swap(up3, down3, far_low, far_high)
    blocks = (block, up1, down1, up2, down2, up3, down3, far_low, far_high, near, outer)
    return copy_call(place_tokens, [(4, 4, rows, width), (2, 8, rows, width)], *blocks)


def place_grads(blocks, pairs):
    row, col = lax.axis_index("row"), lax.axis_index("col")
    core = row % 2
    x, y = col // 4, col % 4
    own_first, own_second = x + core * (y - x), y + core * (x - y)
    places = [(0, 0, 4), (1, 0, 4), (2, 0, 2), (2, 2, 2), (3, 0, 4)]
    for source, (k, start, count) in zip(blocks, places):
        for i in range(count):
            first, second = (own_first + k) % 4, (own_second + start + i) % 4
            there_x, there_y = first + core * (second - first), second + core * (first - second)
            pairs[(there_y + core) % 2, there_x * 2 + there_y // 2] = source[i]


def reduce4(part, half, first):
    low, high, every = slice(0, half), slice(half, 2 * half), slice(0, 2 * half)
    send = lambda k, part: lax.ppermute(part.astype(BF16), ("row", "col"), shift_plane(k, first))
    from_right = send(-1, cat(part(2, low), part(3, high)))
    from_left = send(1, cat(part(1, low), part(2, high)))
    last_low = send(-1, part(3, low) + from_right[low].astype(F32))
    last_high = send(1, part(1, high) + from_left[high].astype(F32))
    near = cat(from_left[low], from_right[high]).astype(F32)
    return part(0, every) + near + cat(last_low, last_high).astype(F32)


def gather4(block, half, first):
    send = lambda k, part: lax.ppermute(part, ("row", "col"), shift_plane(k, first))
    from_right, from_left = send(-1, block), send(1, block)
    return block, from_right, send(-1, from_right[:half]), send(1, from_left[half:]), from_left


def shards(tokens, weight, cotangent):
    row, col = lax.axis_index("row"), lax.axis_index("col")
    z, core = row // 2, row % 2
    x, y = col // 4, col % 4
    a, b = x + core * (y - x), y + core * (x - y)
    rows = tokens.shape[0]
    width, hidden_width = weight.shape

    tiles, token_pairs = gather_tokens(tokens)
    near = [pick(tiles, (a + k) % 4).reshape(4 * rows, width) for k in range(4)]
    summed = reduce4(lambda k, s: dot(near[k][s], weight), 2 * rows, True)
    summed = summed.reshape(4, rows, hidden_width)
    terms = [pick(summed, (b + k) % 4) for k in range(4)]
    pre = reduce4(lambda k, s: terms[k][s], rows // 2, False)
    value, slope = gelu_and_slope(pre)
    hidden = value.astype(BF16)
    grad = (cotangent.astype(F32) * slope).astype(BF16)

    block = cat(*gather4(grad, rows // 2, False)).reshape(4, rows, hidden_width)
    blocks = gather4(block, 2, True)
    (pairs,) = copy_call(place_grads, [(2, 8, rows, hidden_width)], *blocks)
    mine, other = (pairs[i].reshape(8 * rows, hidden_width) for i in range(2))

    away = lax.ppermute(dot_t(other, weight).astype(BF16), "row", SWAP)
    part = (dot_t(mine, weight) + away.astype(F32)).reshape(8, rows, width)
    term = lambda k: pick(part, (z + k) % 8)
    half = rows // 2
    left = lax.ppermute(term(4)[:half].astype(BF16), "row", shift_z(-1))
    right = lax.ppermute(term(4)[half:].astype(BF16), "row", shift_z(1))
    for step in range(3):
        above, below = term(5 + step), term(3 - step)
        if step == 0:
            left = cat((above[:half] + left.astype(F32)).astype(BF16), above[half:].astype(BF16))
            right = cat(below[:half].astype(BF16), (below[half:] + right.astype(F32)).astype(BF16))
        else:
            left = (above + left.astype(F32)).astype(BF16)
            right = (below + right.astype(F32)).astype(BF16)
        left = lax.ppermute(left, "row", shift_z(-1))
        right = lax.ppermute(right, "row", shift_z(1))
    grad_tokens = (term(0) + left.astype(F32) + right.astype(F32)).astype(BF16)

    grad_weight = lax.dot_general(
        token_pairs.reshape(16 * rows, width),
        pairs.reshape(16 * rows, hidden_width),
        (((0,), (0,)), ((), ())),
        preferred_element_type=F32,
    )
    return hidden, grad_weight, grad_tokens


def solution(mesh):
    in_specs = (P("row", "col"), P("col", "row"), P("col", "row"))
    out_specs = (P("col", "row"), P("col", "row"), P("row", "col"))
    return jax.shard_map(shards, mesh=mesh, in_specs=in_specs, out_specs=out_specs, check_vma=False)
```

```python
import math

import jax
import jax.numpy as jnp
from jax import lax
from jax.experimental import pallas as pl
from jax.experimental.pallas import tpu as pltpu
from jax.sharding import PartitionSpec as P

F32, BF16 = jnp.float32, jnp.bfloat16


def gelu_and_slope(value):
    cumulative = 0.5 * (1.0 + jax.scipy.special.erf(value / math.sqrt(2.0)))
    density = jnp.exp(-0.5 * value * value) / math.sqrt(2.0 * math.pi)
    return value * cumulative, cumulative + value * density


def dot(a, b):
    return lax.dot_general(a, b, (((1,), (0,)), ((), ())), preferred_element_type=F32)


def dot_t(a, b):
    return lax.dot_general(a, b, (((1,), (1,)), ((), ())), preferred_element_type=F32)


def shift_plane(k, first):
    pairs = []
    for row in range(16):
        along_x = (row % 2 == 0) == first
        for x in range(4):
            for y in range(4):
                to = (x + k) % 4 * 4 + y if along_x else x * 4 + (y + k) % 4
                pairs.append((row * 16 + x * 4 + y, row * 16 + to))
    return pairs


def shift_z(k):
    return [(z * 2 + c, (z + k) % 8 * 2 + c) for z in range(8) for c in range(2)]


SWAP = [(z * 2 + c, z * 2 + 1 - c) for z in range(8) for c in range(2)]


def cat(*parts):
    return jnp.concatenate(parts, axis=0)


def pick(array, index):
    return lax.dynamic_index_in_dim(array, index, axis=0, keepdims=False)


def copy_call(kernel, out_shapes, *arrays):
    shapes = [jax.ShapeDtypeStruct(shape, BF16) for shape in out_shapes]
    size = 2 * sum(math.prod(s) for s in out_shapes) + 2 * sum(a.size for a in arrays)
    return pl.pallas_call(
        lambda *refs: kernel(refs[: len(arrays)], *refs[len(arrays) :]),
        out_shape=shapes,
        in_specs=[pl.BlockSpec(memory_space=pltpu.VMEM)] * len(arrays),
        out_specs=[pl.BlockSpec(memory_space=pltpu.VMEM)] * len(shapes),
        compiler_params=pltpu.CompilerParams(vmem_limit_bytes=4 * 2**20),
        cost_estimate=pl.CostEstimate(flops=0, bytes_accessed=size, transcendentals=0),
    )(*arrays)


def place_tokens(blocks, tiles, pairs):
    row = lax.axis_index("row")
    z, core = row // 2, row % 2
    rows = tiles.shape[2]
    behind = 2 * core - 1

    def put(value, there, other):
        x, y = there // 2, there % 2 * 2 + (1 - core if other else core)
        tiles[x + core * (y - x), y + core * (x - y)] = value
        pairs[int(other), there] = value

    own, other = blocks[0], blocks[1]
    put(own[...], z, False)
    put(other[...], z, True)
    for k in range(1, 4):
        for source, there, swapped in (
            (blocks[2 * k], (z + 8 + behind * k) % 8, False),
            (blocks[2 * k + 1], (z + 8 - behind * k) % 8, True),
        ):
            put(source[:rows, :], there, swapped)
            put(source[rows:, :], there, not swapped)
    put(blocks[8][...], (z + 4) % 8, False)
    put(blocks[9][...], (z + 4) % 8, True)


def gather_tokens(block):
    rows, width = block.shape
    onward = [
        (z * 2 + c, (z + 1 - 2 * c) % 8 * 2 + c) for z in range(8) for c in range(2)
    ]
    swap = lambda part: lax.ppermute(part, "row", SWAP)
    blocks = [block, swap(block)]
    heard = cat(*blocks)
    for _ in range(3):
        heard = lax.ppermute(heard, "row", onward)
        blocks += [heard, swap(heard)]
    heard = lax.ppermute(heard[:rows], "row", onward)
    blocks += [heard, swap(heard)]
    return copy_call(place_tokens, [(4, 4, rows, width), (2, 8, rows, width)], *blocks)


def place_grads(blocks, pairs):
    row, col = lax.axis_index("row"), lax.axis_index("col")
    core = row % 2
    x, y = col // 4, col % 4
    own_first, own_second = x + core * (y - x), y + core * (x - y)
    places = [(0, 0, 4), (1, 0, 4), (2, 0, 2), (2, 2, 2), (3, 0, 4)]
    for source, (k, start, count) in zip(blocks, places):
        for i in range(count):
            first, second = (own_first + k) % 4, (own_second + start + i) % 4
            there_x, there_y = first + core * (second - first), second + core * (first - second)
            pairs[(there_y + core) % 2, there_x * 2 + there_y // 2] = source[i]


def reduce4(part, half, first):
    low, high, every = slice(0, half), slice(half, 2 * half), slice(0, 2 * half)
    send = lambda k, part: lax.ppermute(part.astype(BF16), ("row", "col"), shift_plane(k, first))
    from_right = send(-1, cat(part(2, low), part(3, high)))
    from_left = send(1, cat(part(1, low), part(2, high)))
    last_low = send(-1, part(3, low) + from_right[low].astype(F32))
    last_high = send(1, part(1, high) + from_left[high].astype(F32))
    near = cat(from_left[low], from_right[high]).astype(F32)
    return part(0, every) + near + cat(last_low, last_high).astype(F32)


def gather4(block, half, first):
    send = lambda k, part: lax.ppermute(part, ("row", "col"), shift_plane(k, first))
    from_right, from_left = send(-1, block), send(1, block)
    return block, from_right, send(-1, from_right[:half]), send(1, from_left[half:]), from_left


def shards(tokens, weight, cotangent):
    row, col = lax.axis_index("row"), lax.axis_index("col")
    z, core = row // 2, row % 2
    x, y = col // 4, col % 4
    a, b = x + core * (y - x), y + core * (x - y)
    rows = tokens.shape[0]
    width, hidden_width = weight.shape

    tiles, token_pairs = gather_tokens(tokens)
    near = [pick(tiles, (a + k) % 4).reshape(4 * rows, width) for k in range(4)]
    summed = reduce4(lambda k, s: dot(near[k][s], weight), 2 * rows, True)
    summed = summed.reshape(4, rows, hidden_width)
    terms = [pick(summed, (b + k) % 4) for k in range(4)]
    pre = reduce4(lambda k, s: terms[k][s], rows // 2, False)
    value, slope = gelu_and_slope(pre)
    hidden = value.astype(BF16)
    grad = (cotangent.astype(F32) * slope).astype(BF16)

    block = cat(*gather4(grad, rows // 2, False)).reshape(4, rows, hidden_width)
    blocks = gather4(block, 2, True)
    (pairs,) = copy_call(place_grads, [(2, 8, rows, hidden_width)], *blocks)
    mine, other = (pairs[i].reshape(8 * rows, hidden_width) for i in range(2))

    away = lax.ppermute(dot_t(other, weight).astype(BF16), "row", SWAP)
    away = away.reshape(8, rows, width)
    part = dot_t(mine, weight).reshape(8, rows, width)

    def term(k):
        there = (z + k) % 8
        return pick(part, there) + pick(away, there).astype(F32)

    half = rows // 2
    left = lax.ppermute(term(4)[:half].astype(BF16), "row", shift_z(-1))
    right = lax.ppermute(term(4)[half:].astype(BF16), "row", shift_z(1))
    for step in range(3):
        above, below = term(5 + step), term(3 - step)
        if step == 0:
            left = cat((above[:half] + left.astype(F32)).astype(BF16), above[half:].astype(BF16))
            right = cat(below[:half].astype(BF16), (below[half:] + right.astype(F32)).astype(BF16))
        else:
            left = (above + left.astype(F32)).astype(BF16)
            right = (below + right.astype(F32)).astype(BF16)
        left = lax.ppermute(left, "row", shift_z(-1))
        right = lax.ppermute(right, "row", shift_z(1))
    grad_tokens = (term(0) + left.astype(F32) + right.astype(F32)).astype(BF16)

    other, mine = (
        lax.dot_general(
            token_pairs[i].reshape(8 * rows, width),
            pairs[i].reshape(8 * rows, hidden_width),
            (((0,), (0,)), ((), ())),
            preferred_element_type=F32,
        )
        for i in (1, 0)
    )
    grad_weight = other + mine
    return hidden, grad_weight, grad_tokens


def solution(mesh):
    in_specs = (P("row", "col"), P("col", "row"), P("col", "row"))
    out_specs = (P("col", "row"), P("col", "row"), P("row", "col"))
    return jax.shard_map(shards, mesh=mesh, in_specs=in_specs, out_specs=out_specs, check_vma=False)
```

```python
import math

import jax
import jax.numpy as jnp
from jax import lax
from jax.experimental import pallas as pl
from jax.experimental.pallas import tpu as pltpu
from jax.sharding import PartitionSpec as P

F32, BF16 = jnp.float32, jnp.bfloat16
CHUNKS = 2


def gelu_and_slope(value):
    cumulative = 0.5 * (1.0 + jax.scipy.special.erf(value / math.sqrt(2.0)))
    density = jnp.exp(-0.5 * value * value) / math.sqrt(2.0 * math.pi)
    return value * cumulative, cumulative + value * density


def dot(a, b):
    return lax.dot_general(a, b, (((a.ndim - 1,), (0,)), ((), ())), preferred_element_type=F32)


def dot_t(a, b):
    return lax.dot_general(a, b, (((a.ndim - 1,), (1,)), ((), ())), preferred_element_type=F32)


def shift_x(k):
    return [(x * 4 + y, (x + k) % 4 * 4 + y) for x in range(4) for y in range(4)]


def shift_y(k):
    return [(x * 4 + y, x * 4 + (y + k) % 4) for x in range(4) for y in range(4)]


def shift_z(k):
    return [(z * 2 + c, (z + k) % 8 * 2 + c) for z in range(8) for c in range(2)]


SWAP = [(z * 2 + c, z * 2 + 1 - c) for z in range(8) for c in range(2)]


def cat(*parts):
    return jnp.concatenate(parts, axis=0)


def from_relative(blocks, me):
    n = len(blocks)
    twice = jnp.stack(blocks + blocks[:-1])
    return lax.dynamic_slice_in_dim(twice, (n - me) % n, n, axis=0)


def pick(array, index):
    return lax.dynamic_index_in_dim(array, index, axis=0, keepdims=False)


def place_kernel(count, *refs):
    blocks, first, second = refs[:count], refs[count], refs[count + 1]
    row = lax.axis_index("row")
    z, core = row // 2, row % 2
    half = first.shape[2]

    def put(target, value, k, parity):
        there = (z + k) % 8
        x, y = there // 2, there % 2 * 2 + parity
        target[(x, y) if target is first else (y, x)] = value

    distances = [[0], [7], [1], [6], [2], [5], [3], [0, 7, 1, 6, 2], [5, 3, 4]]
    for n, ks in enumerate(distances):
        for i, k in enumerate(ks):
            for part, target in enumerate((first, second)):
                value = blocks[n][pl.ds((2 * i + part) * half, half), :]
                put(target, value, k, core if n < 7 else 1 - core)
    put(first, blocks[9][...], 4, core)
    put(second, blocks[10][...], 4, core)


def gather_tokens(block):
    half, width = block.shape[0] // 2, block.shape[1]
    swap = lambda *parts: lax.ppermute(cat(*parts), "row", SWAP)
    above = lambda part: lax.ppermute(part, "row", shift_z(1))
    below = lambda part: lax.ppermute(part, "row", shift_z(-1))
    up1, down1 = above(block), below(block)
    up2, down2 = above(up1), below(down1)
    up3, down3 = above(up2), below(down2)
    near = swap(block, up1, down1, up2, down2)
    far_low, far_high = above(up3[:half]), below(down3[half:])
    outer = swap(up3, down3, far_low, far_high)
    blocks = [block, up1, down1, up2, down2, up3, down3, near, outer, far_low, far_high]
    shape = jax.ShapeDtypeStruct((4, 4, half, width), block.dtype)
    return pl.pallas_call(
        lambda *refs: place_kernel(len(blocks), *refs),
        out_shape=(shape, shape),
        in_specs=[pl.BlockSpec(memory_space=pltpu.VMEM)] * len(blocks),
        out_specs=(pl.BlockSpec(memory_space=pltpu.VMEM),) * 2,
        compiler_params=pltpu.CompilerParams(vmem_limit_bytes=4 * 2**20),
        cost_estimate=pl.CostEstimate(flops=0, bytes_accessed=128 * half * width, transcendentals=0),
        name="place_tokens",
    )(*blocks)


def reduce4(part, half, shift):
    low, high, every = slice(0, half), slice(half, 2 * half), slice(0, 2 * half)
    leftward = lambda part: lax.ppermute(part.astype(BF16), "col", shift(-1))
    rightward = lambda part: lax.ppermute(part.astype(BF16), "col", shift(1))
    from_right = leftward(cat(part(2, low), part(3, high)))
    from_left = rightward(cat(part(1, low), part(2, high)))
    last_low = leftward(part(3, low) + from_right[low].astype(F32))
    last_high = rightward(part(1, high) + from_left[high].astype(F32))
    near = cat(from_left[low], from_right[high]).astype(F32)
    return part(0, every) + near + cat(last_low, last_high).astype(F32)


def gather4(block, half, shift):
    leftward = lambda part: lax.ppermute(part, "col", shift(-1))
    rightward = lambda part: lax.ppermute(part, "col", shift(1))
    from_right, from_left = leftward(block), rightward(block)
    far = cat(leftward(from_right[:half]), rightward(from_left[half:]))
    return [block, from_right, far, from_left]


def shards(tokens, weight, cotangent):
    row, col = lax.axis_index("row"), lax.axis_index("col")
    z, core = row // 2, row % 2
    x, y = col // 4, col % 4
    rows = tokens.shape[0] // CHUNKS
    width, hidden_width = weight.shape

    gathered = gather_tokens(tokens)
    hiddens, grads = [], []
    for u in range(CHUNKS):
        full = gathered[u]
        (a, shift_a), (b, shift_b) = ((x, shift_x), (y, shift_y))[:: 1 if u % 2 == 0 else -1]
        near = [pick(full, (a + k) % 4) for k in range(4)]
        near = [n.reshape(4 * rows, width) for n in near]
        summed = reduce4(lambda k, s: dot(near[k][s], weight), 2 * rows, shift_a)
        summed = summed.reshape(4, rows, hidden_width)
        terms = [pick(summed, (b + k) % 4) for k in range(4)]
        pre = reduce4(lambda k, s: terms[k][s], rows // 2, shift_b)
        value, slope = gelu_and_slope(pre)
        hiddens.append(value.astype(BF16))
        grad = (cotangent[u * rows : (u + 1) * rows].astype(F32) * slope).astype(BF16)
        block = from_relative(gather4(grad, rows // 2, shift_b), b)
        block = gather4(block.reshape(4 * rows, hidden_width), 2 * rows, shift_a)
        grads.append(from_relative(block, a).reshape(4, 4, rows, hidden_width))

    terms, grad_weight = [], None
    for u in range(CHUNKS):
        if u % 2 == 0:
            parity = grads[u].reshape(8, 2, rows, hidden_width)
        else:
            parity = grads[u].reshape(2, 2, 4, rows, hidden_width)
        mine, other = (
            lax.dynamic_index_in_dim(parity, c, 1, False).reshape(8 * rows, hidden_width)
            for c in (core, 1 - core)
        )
        away = lax.ppermute(dot_t(other, weight).astype(BF16), "row", SWAP)
        away = away.reshape(8, rows, width)
        part = lax.optimization_barrier(dot_t(mine, weight).reshape(8, rows, width))
        terms.append((part, away))

    def term(k):
        there = (z + k) % 8
        places = there, there % 2 * 4 + there // 2
        return [pick(part, p) + pick(away, p).astype(F32) for (part, away), p in zip(terms, places)]

    left = lax.ppermute(term(4)[0].astype(BF16), "row", shift_z(-1))
    right = lax.ppermute(term(4)[1].astype(BF16), "row", shift_z(1))
    for step in range(3):
        first, second = term(5 + step)
        if step == 0:
            left = cat((first + left.astype(F32)).astype(BF16), second.astype(BF16))
        else:
            left = (cat(first, second) + left.astype(F32)).astype(BF16)
        first, second = term(3 - step)
        if step == 0:
            right = cat(first.astype(BF16), (second + right.astype(F32)).astype(BF16))
        else:
            right = (cat(first, second) + right.astype(F32)).astype(BF16)
        left = lax.ppermute(left, "row", shift_z(-1))
        right = lax.ppermute(right, "row", shift_z(1))
    grad_tokens = cat(*term(0)) + left.astype(F32) + right.astype(F32)
    for u in range(CHUNKS):
        product = lax.dot_general(
            gathered[u].reshape(-1, width),
            grads[u].reshape(-1, hidden_width),
            (((0,), (0,)), ((), ())),
            preferred_element_type=F32,
        )
        grad_weight = product if grad_weight is None else grad_weight + product
    return cat(*hiddens), grad_weight, grad_tokens.astype(BF16)


def solution(mesh):
    in_specs = (P("row", "col"), P("col", "row"), P("col", "row"))
    out_specs = (P("col", "row"), P("col", "row"), P("row", "col"))
    return jax.shard_map(shards, mesh=mesh, in_specs=in_specs, out_specs=out_specs, check_vma=False)
```

```python
import math

import jax
import jax.numpy as jnp
from jax import lax
from jax.experimental import pallas as pl
from jax.experimental.pallas import tpu as pltpu
from jax.sharding import PartitionSpec as P

F32, BF16 = jnp.float32, jnp.bfloat16
CHUNKS = 2


def gelu_and_slope(value):
    cumulative = 0.5 * (1.0 + jax.scipy.special.erf(value / math.sqrt(2.0)))
    density = jnp.exp(-0.5 * value * value) / math.sqrt(2.0 * math.pi)
    return value * cumulative, cumulative + value * density


def dot(a, b):
    return lax.dot_general(a, b, (((a.ndim - 1,), (0,)), ((), ())), preferred_element_type=F32)


def dot_t(a, b):
    return lax.dot_general(a, b, (((a.ndim - 1,), (1,)), ((), ())), preferred_element_type=F32)


def shift_x(k):
    return [(x * 4 + y, (x + k) % 4 * 4 + y) for x in range(4) for y in range(4)]


def shift_y(k):
    return [(x * 4 + y, x * 4 + (y + k) % 4) for x in range(4) for y in range(4)]


def shift_z(k):
    return [(z * 2 + c, (z + k) % 8 * 2 + c) for z in range(8) for c in range(2)]


SWAP = [(z * 2 + c, z * 2 + 1 - c) for z in range(8) for c in range(2)]


def cat(*parts):
    return jnp.concatenate(parts, axis=0)


def from_relative(blocks, me):
    n = len(blocks)
    twice = jnp.stack(blocks + blocks[:-1])
    return lax.dynamic_slice_in_dim(twice, (n - me) % n, n, axis=0)


def pick(array, index):
    return lax.dynamic_index_in_dim(array, index, axis=0, keepdims=False)


def place(blocks, whose, targets, half, width):
    count, kept = len(blocks), 0 if targets is None else 2

    def kernel(*refs):
        first, second = refs[count + kept :]
        row = lax.axis_index("row")
        z, core = row // 2, row % 2
        for ref, places in zip(refs, whose):
            start = 0
            for k, other, part in places:
                there = (z + k) % 8
                x, y = there // 2, there % 2 * 2 + (1 - core if other else core)
                if part != 1:
                    first[x, y] = ref[pl.ds(start, half), :]
                    start += half
                if part != 0:
                    second[y, x] = ref[pl.ds(start, half), :]
                    start += half

    shape = jax.ShapeDtypeStruct((4, 4, half, width), BF16)
    return pl.pallas_call(
        kernel,
        out_shape=(shape, shape),
        in_specs=[pl.BlockSpec(memory_space=pltpu.VMEM)] * (count + kept),
        out_specs=(pl.BlockSpec(memory_space=pltpu.VMEM),) * 2,
        input_output_aliases={count + i: i for i in range(kept)},
        compiler_params=pltpu.CompilerParams(vmem_limit_bytes=4 * 2**20),
        cost_estimate=pl.CostEstimate(
            flops=0, bytes_accessed=4 * sum(b.size for b in blocks), transcendentals=0
        ),
        name="place_tokens",
    )(*blocks, *(targets or ()))


def gather_tokens(block):
    half, width = block.shape[0] // 2, block.shape[1]
    swap = lambda *parts: lax.ppermute(cat(*parts), "row", SWAP)
    above = lambda part: lax.ppermute(part, "row", shift_z(1))
    below = lambda part: lax.ppermute(part, "row", shift_z(-1))
    up1, down1 = above(block), below(block)
    up2, down2 = above(up1), below(down1)
    up3, down3 = above(up2), below(down2)
    near = swap(block, up1, down1, up2, down2)
    far_low, far_high = above(up3[:half]), below(down3[half:])
    outer = swap(up3, down3)
    last = swap(far_low, far_high)
    blocks = [block, up1, down1, up2, down2, up3, down3, near]
    whose = [[(k, False, None)] for k in (0, 7, 1, 6, 2, 5, 3)] + [[(k, True, None) for k in (0, 7, 1, 6, 2)]]
    placed = place(blocks, whose, None, half, width)
    whose = [[(5, True, None), (3, True, None)], [(4, False, 0)], [(4, False, 1)], [(4, True, None)]]
    return place([outer, far_low, far_high, last], whose, placed, half, width)


def activate(sums, cotangent):
    def kernel(own, from_left, from_right, last_low, last_high, cotangent, hidden, grad):
        half = last_low.shape[0]
        for part, near, last in ((0, from_left, last_low), (1, from_right, last_high)):
            rows = slice(part * half, (part + 1) * half)
            pre = own[rows, :] + near[rows, :].astype(F32) + last[...].astype(F32)
            value, slope = gelu_and_slope(pre)
            hidden[rows, :] = value.astype(BF16)
            grad[rows, :] = (cotangent[rows, :].astype(F32) * slope).astype(BF16)

    shape = jax.ShapeDtypeStruct(cotangent.shape, BF16)
    return pl.pallas_call(
        kernel,
        out_shape=(shape, shape),
        in_specs=[pl.BlockSpec(memory_space=pltpu.VMEM)] * 6,
        out_specs=(pl.BlockSpec(memory_space=pltpu.VMEM),) * 2,
        compiler_params=pltpu.CompilerParams(vmem_limit_bytes=8 * 2**20),
        cost_estimate=pl.CostEstimate(
            flops=60 * cotangent.size, bytes_accessed=16 * cotangent.size, transcendentals=cotangent.size
        ),
        name="activate",
    )(*sums, cotangent)


def reduce4(part, half, shift):
    low, high, every = slice(0, half), slice(half, 2 * half), slice(0, 2 * half)
    leftward = lambda part: lax.ppermute(part.astype(BF16), "col", shift(-1))
    rightward = lambda part: lax.ppermute(part.astype(BF16), "col", shift(1))
    from_right = leftward(cat(part(2, low), part(3, high)))
    from_left = rightward(cat(part(1, low), part(2, high)))
    last_low = leftward(part(3, low) + from_right[low].astype(F32))
    last_high = rightward(part(1, high) + from_left[high].astype(F32))
    return part(0, every), from_left, from_right, last_low, last_high


def total4(own, from_left, from_right, last_low, last_high):
    half = last_low.shape[0]
    near = cat(from_left[:half], from_right[half:]).astype(F32)
    return own + near + cat(last_low, last_high).astype(F32)


def gather4(block, half, shift):
    leftward = lambda part: lax.ppermute(part, "col", shift(-1))
    rightward = lambda part: lax.ppermute(part, "col", shift(1))
    from_right, from_left = leftward(block), rightward(block)
    far = cat(leftward(from_right[:half]), rightward(from_left[half:]))
    return [block, from_right, far, from_left]


def shards(tokens, weight, cotangent):
    row, col = lax.axis_index("row"), lax.axis_index("col")
    z, core = row // 2, row % 2
    x, y = col // 4, col % 4
    rows = tokens.shape[0] // CHUNKS
    width, hidden_width = weight.shape

    gathered = gather_tokens(tokens)
    hiddens, grads = [], []
    for u in range(CHUNKS):
        full = gathered[u]
        (a, shift_a), (b, shift_b) = ((x, shift_x), (y, shift_y))[:: 1 if u % 2 == 0 else -1]
        near = [pick(full, (a + k) % 4) for k in range(4)]
        near = [n.reshape(4 * rows, width) for n in near]
        summed = total4(*reduce4(lambda k, s: dot(near[k][s], weight), 2 * rows, shift_a))
        summed = summed.reshape(4, rows, hidden_width)
        terms = [pick(summed, (b + k) % 4) for k in range(4)]
        sums = reduce4(lambda k, s: terms[k][s], rows // 2, shift_b)
        hidden, grad = activate(sums, cotangent[u * rows : (u + 1) * rows])
        hiddens.append(hidden)
        block = from_relative(gather4(grad, rows // 2, shift_b), b)
        block = gather4(block.reshape(4 * rows, hidden_width), 2 * rows, shift_a)
        grads.append(from_relative(block, a).reshape(4, 4, rows, hidden_width))

    terms, grad_weight = [], None
    for u in range(CHUNKS):
        if u % 2 == 0:
            parity = grads[u].reshape(8, 2, rows, hidden_width)
        else:
            parity = grads[u].reshape(2, 2, 4, rows, hidden_width)
        mine, other = (
            lax.dynamic_index_in_dim(parity, c, 1, False).reshape(8 * rows, hidden_width)
            for c in (core, 1 - core)
        )
        away = lax.ppermute(dot_t(other, weight).astype(BF16), "row", SWAP)
        away = away.reshape(8, rows, width)
        part = lax.optimization_barrier(dot_t(mine, weight).reshape(8, rows, width))
        terms.append((part, away))

    def term(k):
        there = (z + k) % 8
        places = there, there % 2 * 4 + there // 2
        return [pick(part, p) + pick(away, p).astype(F32) for (part, away), p in zip(terms, places)]

    left = lax.ppermute(term(4)[0].astype(BF16), "row", shift_z(-1))
    right = lax.ppermute(term(4)[1].astype(BF16), "row", shift_z(1))
    for step in range(3):
        first, second = term(5 + step)
        if step == 0:
            left = cat((first + left.astype(F32)).astype(BF16), second.astype(BF16))
        else:
            left = (cat(first, second) + left.astype(F32)).astype(BF16)
        first, second = term(3 - step)
        if step == 0:
            right = cat(first.astype(BF16), (second + right.astype(F32)).astype(BF16))
        else:
            right = (cat(first, second) + right.astype(F32)).astype(BF16)
        left = lax.ppermute(left, "row", shift_z(-1))
        right = lax.ppermute(right, "row", shift_z(1))
    grad_tokens = cat(*term(0)) + left.astype(F32) + right.astype(F32)
    for u in range(CHUNKS):
        product = lax.dot_general(
            gathered[u].reshape(-1, width),
            grads[u].reshape(-1, hidden_width),
            (((0,), (0,)), ((), ())),
            preferred_element_type=F32,
        )
        grad_weight = product if grad_weight is None else grad_weight + product
    return cat(*hiddens), grad_weight, grad_tokens.astype(BF16)


def solution(mesh):
    in_specs = (P("row", "col"), P("col", "row"), P("col", "row"))
    out_specs = (P("col", "row"), P("col", "row"), P("row", "col"))
    return jax.shard_map(shards, mesh=mesh, in_specs=in_specs, out_specs=out_specs, check_vma=False)
```

```python
import math

import jax
import jax.numpy as jnp
from jax import lax
from jax.experimental import pallas as pl
from jax.experimental.pallas import tpu as pltpu
from jax.sharding import PartitionSpec as P

F32, BF16 = jnp.float32, jnp.bfloat16
CHUNKS = 2


def gelu_and_slope(value):
    cumulative = 0.5 * (1.0 + jax.scipy.special.erf(value / math.sqrt(2.0)))
    density = jnp.exp(-0.5 * value * value) / math.sqrt(2.0 * math.pi)
    return value * cumulative, cumulative + value * density


def dot(a, b):
    return lax.dot_general(a, b, (((a.ndim - 1,), (0,)), ((), ())), preferred_element_type=F32)


def dot_t(a, b):
    return lax.dot_general(a, b, (((a.ndim - 1,), (1,)), ((), ())), preferred_element_type=F32)


def shift_x(k):
    return [(x * 4 + y, (x + k) % 4 * 4 + y) for x in range(4) for y in range(4)]


def shift_y(k):
    return [(x * 4 + y, x * 4 + (y + k) % 4) for x in range(4) for y in range(4)]


def shift_z(k):
    return [(z * 2 + c, (z + k) % 8 * 2 + c) for z in range(8) for c in range(2)]


SWAP = [(z * 2 + c, z * 2 + 1 - c) for z in range(8) for c in range(2)]


def cat(*parts):
    return jnp.concatenate(parts, axis=0)


def pick(array, index):
    return lax.dynamic_index_in_dim(array, index, axis=0, keepdims=False)


def place_kernel(count, *refs):
    blocks, first, second = refs[:count], refs[count], refs[count + 1]
    row = lax.axis_index("row")
    z, core = row // 2, row % 2
    half = first.shape[2]

    def put(target, value, k, parity):
        there = (z + k) % 8
        x, y = there // 2, there % 2 * 2 + parity
        target[(x, y) if target is first else (y, x)] = value

    distances = [[0], [7], [1], [6], [2], [5], [3], [0, 7, 1, 6, 2], [5, 3, 4]]
    for n, ks in enumerate(distances):
        for i, k in enumerate(ks):
            for part, target in enumerate((first, second)):
                value = blocks[n][pl.ds((2 * i + part) * half, half), :]
                put(target, value, k, core if n < 7 else 1 - core)
    put(first, blocks[9][...], 4, core)
    put(second, blocks[10][...], 4, core)


def gather_tokens(block):
    half, width = block.shape[0] // 2, block.shape[1]
    swap = lambda *parts: lax.ppermute(cat(*parts), "row", SWAP)
    above = lambda part: lax.ppermute(part, "row", shift_z(1))
    below = lambda part: lax.ppermute(part, "row", shift_z(-1))
    up1, down1 = above(block), below(block)
    up2, down2 = above(up1), below(down1)
    up3, down3 = above(up2), below(down2)
    near = swap(block, up1, down1, up2, down2)
    far_low, far_high = above(up3[:half]), below(down3[half:])
    outer = swap(up3, down3, far_low, far_high)
    blocks = [block, up1, down1, up2, down2, up3, down3, near, outer, far_low, far_high]
    shape = jax.ShapeDtypeStruct((4, 4, half, width), block.dtype)
    return pl.pallas_call(
        lambda *refs: place_kernel(len(blocks), *refs),
        out_shape=(shape, shape),
        in_specs=[pl.BlockSpec(memory_space=pltpu.VMEM)] * len(blocks),
        out_specs=(pl.BlockSpec(memory_space=pltpu.VMEM),) * 2,
        compiler_params=pltpu.CompilerParams(vmem_limit_bytes=4 * 2**20),
        cost_estimate=pl.CostEstimate(flops=0, bytes_accessed=128 * half * width, transcendentals=0),
        name="place_tokens",
    )(*blocks)


def activate(sums, cotangent):
    def kernel(own, from_left, from_right, last_low, last_high, cotangent, hidden, grad):
        half = last_low.shape[0]
        for part, near, last in ((0, from_left, last_low), (1, from_right, last_high)):
            rows = slice(part * half, (part + 1) * half)
            pre = own[rows, :] + near[rows, :].astype(F32) + last[...].astype(F32)
            value, slope = gelu_and_slope(pre)
            hidden[rows, :] = value.astype(BF16)
            grad[rows, :] = (cotangent[rows, :].astype(F32) * slope).astype(BF16)

    shape = jax.ShapeDtypeStruct(cotangent.shape, BF16)
    return pl.pallas_call(
        kernel,
        out_shape=(shape, shape),
        in_specs=[pl.BlockSpec(memory_space=pltpu.VMEM)] * 6,
        out_specs=(pl.BlockSpec(memory_space=pltpu.VMEM),) * 2,
        compiler_params=pltpu.CompilerParams(vmem_limit_bytes=8 * 2**20),
        cost_estimate=pl.CostEstimate(
            flops=60 * cotangent.size, bytes_accessed=16 * cotangent.size, transcendentals=cotangent.size
        ),
        name="activate",
    )(*sums, cotangent)


def reduce4(part, half, shift):
    low, high, every = slice(0, half), slice(half, 2 * half), slice(0, 2 * half)
    leftward = lambda part: lax.ppermute(part.astype(BF16), "col", shift(-1))
    rightward = lambda part: lax.ppermute(part.astype(BF16), "col", shift(1))
    from_right = leftward(cat(part(2, low), part(3, high)))
    from_left = rightward(cat(part(1, low), part(2, high)))
    last_low = leftward(part(3, low) + from_right[low].astype(F32))
    last_high = rightward(part(1, high) + from_left[high].astype(F32))
    return part(0, every), from_left, from_right, last_low, last_high


def total4(own, from_left, from_right, last_low, last_high):
    half = last_low.shape[0]
    near = cat(from_left[:half], from_right[half:]).astype(F32)
    return own + near + cat(last_low, last_high).astype(F32)


def gather4(block, half, shift):
    leftward = lambda part: lax.ppermute(part, "col", shift(-1))
    rightward = lambda part: lax.ppermute(part, "col", shift(1))
    from_right, from_left = leftward(block), rightward(block)
    return block, from_right, leftward(from_right[:half]), rightward(from_left[half:]), from_left


def place_grads(blocks, rows, transposed):
    def kernel(own, right, far_low, far_high, left, target):
        col = lax.axis_index("col")
        first, second = (col % 4, col // 4) if transposed else (col // 4, col % 4)
        for ref, k, start, count in ((own, 0, 0, 4), (right, 1, 0, 4), (far_low, 2, 0, 2), (far_high, 2, 2, 2), (left, 3, 0, 4)):
            for i in range(count):
                target[(first + k) % 4, (second + start + i) % 4] = ref[pl.ds(i * rows, rows), :]

    width = blocks[0].shape[1]
    return pl.pallas_call(
        kernel,
        out_shape=jax.ShapeDtypeStruct((4, 4, rows, width), BF16),
        in_specs=[pl.BlockSpec(memory_space=pltpu.VMEM)] * 5,
        out_specs=pl.BlockSpec(memory_space=pltpu.VMEM),
        compiler_params=pltpu.CompilerParams(vmem_limit_bytes=4 * 2**20),
        cost_estimate=pl.CostEstimate(flops=0, bytes_accessed=64 * rows * width, transcendentals=0),
        name="place_grads",
    )(*blocks)


def shards(tokens, weight, cotangent):
    row, col = lax.axis_index("row"), lax.axis_index("col")
    z, core = row // 2, row % 2
    x, y = col // 4, col % 4
    rows = tokens.shape[0] // CHUNKS
    width, hidden_width = weight.shape

    gathered = gather_tokens(tokens)
    hiddens, grads = [], []
    for u in range(CHUNKS):
        full = gathered[u]
        (a, shift_a), (b, shift_b) = ((x, shift_x), (y, shift_y))[:: 1 if u % 2 == 0 else -1]
        near = [pick(full, (a + k) % 4) for k in range(4)]
        near = [n.reshape(4 * rows, width) for n in near]
        summed = total4(*reduce4(lambda k, s: dot(near[k][s], weight), 2 * rows, shift_a))
        summed = summed.reshape(4, rows, hidden_width)
        terms = [pick(summed, (b + k) % 4) for k in range(4)]
        sums = reduce4(lambda k, s: terms[k][s], rows // 2, shift_b)
        hidden, grad = activate(sums, cotangent[u * rows : (u + 1) * rows])
        hiddens.append(hidden)
        block = cat(*gather4(grad, rows // 2, shift_b))
        grads.append(place_grads(gather4(block, 2 * rows, shift_a), rows, u % 2 == 1))

    terms, grad_weight = [], None
    for u in range(CHUNKS):
        if u % 2 == 0:
            parity = grads[u].reshape(8, 2, rows, hidden_width)
        else:
            parity = grads[u].reshape(2, 2, 4, rows, hidden_width)
        mine, other = (
            lax.dynamic_index_in_dim(parity, c, 1, False).reshape(8 * rows, hidden_width)
            for c in (core, 1 - core)
        )
        away = lax.ppermute(dot_t(other, weight).astype(BF16), "row", SWAP)
        away = away.reshape(8, rows, width)
        part = lax.optimization_barrier(dot_t(mine, weight).reshape(8, rows, width))
        terms.append((part, away))

    def term(k):
        there = (z + k) % 8
        places = there, there % 2 * 4 + there // 2
        return [pick(part, p) + pick(away, p).astype(F32) for (part, away), p in zip(terms, places)]

    left = lax.ppermute(term(4)[0].astype(BF16), "row", shift_z(-1))
    right = lax.ppermute(term(4)[1].astype(BF16), "row", shift_z(1))
    for step in range(3):
        first, second = term(5 + step)
        if step == 0:
            left = cat((first + left.astype(F32)).astype(BF16), second.astype(BF16))
        else:
            left = (cat(first, second) + left.astype(F32)).astype(BF16)
        first, second = term(3 - step)
        if step == 0:
            right = cat(first.astype(BF16), (second + right.astype(F32)).astype(BF16))
        else:
            right = (cat(first, second) + right.astype(F32)).astype(BF16)
        left = lax.ppermute(left, "row", shift_z(-1))
        right = lax.ppermute(right, "row", shift_z(1))
    grad_tokens = cat(*term(0)) + left.astype(F32) + right.astype(F32)
    for u in range(CHUNKS):
        product = lax.dot_general(
            gathered[u].reshape(-1, width),
            grads[u].reshape(-1, hidden_width),
            (((0,), (0,)), ((), ())),
            preferred_element_type=F32,
        )
        grad_weight = product if grad_weight is None else grad_weight + product
    return cat(*hiddens), grad_weight, grad_tokens.astype(BF16)


def solution(mesh):
    in_specs = (P("row", "col"), P("col", "row"), P("col", "row"))
    out_specs = (P("col", "row"), P("col", "row"), P("row", "col"))
    return jax.shard_map(shards, mesh=mesh, in_specs=in_specs, out_specs=out_specs, check_vma=False)
```

```python
import math

import jax
import jax.numpy as jnp
from jax import lax
from jax.experimental import pallas as pl
from jax.experimental.pallas import tpu as pltpu
from jax.sharding import PartitionSpec as P

F32, BF16 = jnp.float32, jnp.bfloat16
CHUNKS = 2


def gelu_and_slope(value):
    cumulative = 0.5 * (1.0 + jax.scipy.special.erf(value / math.sqrt(2.0)))
    density = jnp.exp(-0.5 * value * value) / math.sqrt(2.0 * math.pi)
    return value * cumulative, cumulative + value * density


def dot(a, b):
    return lax.dot_general(a, b, (((a.ndim - 1,), (0,)), ((), ())), preferred_element_type=F32)


def dot_t(a, b):
    return lax.dot_general(a, b, (((a.ndim - 1,), (1,)), ((), ())), preferred_element_type=F32)


def shift_x(k):
    return [(x * 4 + y, (x + k) % 4 * 4 + y) for x in range(4) for y in range(4)]


def shift_y(k):
    return [(x * 4 + y, x * 4 + (y + k) % 4) for x in range(4) for y in range(4)]


def shift_z(k):
    return [(z * 2 + c, (z + k) % 8 * 2 + c) for z in range(8) for c in range(2)]


SWAP = [(z * 2 + c, z * 2 + 1 - c) for z in range(8) for c in range(2)]


def cat(*parts):
    return jnp.concatenate(parts, axis=0)


def pick(array, index):
    return lax.dynamic_index_in_dim(array, index, axis=0, keepdims=False)


def place_kernel(count, *refs):
    blocks, first, second = refs[:count], refs[count], refs[count + 1]
    row = lax.axis_index("row")
    z, core = row // 2, row % 2
    half = first.shape[2]

    def put(target, value, k, parity):
        there = (z + k) % 8
        x, y = there // 2, there % 2 * 2 + parity
        target[(x, y) if target is first else (y, x)] = value

    distances = [[0], [7], [1], [6], [2], [5], [3], [0, 7, 1, 6, 2], [5, 3, 4]]
    for n, ks in enumerate(distances):
        for i, k in enumerate(ks):
            for part, target in enumerate((first, second)):
                value = blocks[n][pl.ds((2 * i + part) * half, half), :]
                put(target, value, k, core if n < 7 else 1 - core)
    put(first, blocks[9][...], 4, core)
    put(second, blocks[10][...], 4, core)


def gather_tokens(block):
    half, width = block.shape[0] // 2, block.shape[1]
    swap = lambda *parts: lax.ppermute(cat(*parts), "row", SWAP)
    above = lambda part: lax.ppermute(part, "row", shift_z(1))
    below = lambda part: lax.ppermute(part, "row", shift_z(-1))
    up1, down1 = above(block), below(block)
    up2, down2 = above(up1), below(down1)
    up3, down3 = above(up2), below(down2)
    near = swap(block, up1, down1, up2, down2)
    far_low, far_high = above(up3[:half]), below(down3[half:])
    outer = swap(up3, down3, far_low, far_high)
    blocks = [block, up1, down1, up2, down2, up3, down3, near, outer, far_low, far_high]
    shape = jax.ShapeDtypeStruct((4, 4, half, width), block.dtype)
    return pl.pallas_call(
        lambda *refs: place_kernel(len(blocks), *refs),
        out_shape=(shape, shape),
        in_specs=[pl.BlockSpec(memory_space=pltpu.VMEM)] * len(blocks),
        out_specs=(pl.BlockSpec(memory_space=pltpu.VMEM),) * 2,
        compiler_params=pltpu.CompilerParams(vmem_limit_bytes=4 * 2**20),
        cost_estimate=pl.CostEstimate(flops=0, bytes_accessed=128 * half * width, transcendentals=0),
        name="place_tokens",
    )(*blocks)


def activate(sums, cotangent):
    def kernel(own, from_left, from_right, last_low, last_high, cotangent, hidden, grad):
        half = last_low.shape[0]
        for part, near, last in ((0, from_left, last_low), (1, from_right, last_high)):
            rows = slice(part * half, (part + 1) * half)
            pre = own[rows, :] + near[rows, :].astype(F32) + last[...].astype(F32)
            value, slope = gelu_and_slope(pre)
            hidden[rows, :] = value.astype(BF16)
            grad[rows, :] = (cotangent[rows, :].astype(F32) * slope).astype(BF16)

    shape = jax.ShapeDtypeStruct(cotangent.shape, BF16)
    return pl.pallas_call(
        kernel,
        out_shape=(shape, shape),
        in_specs=[pl.BlockSpec(memory_space=pltpu.VMEM)] * 6,
        out_specs=(pl.BlockSpec(memory_space=pltpu.VMEM),) * 2,
        compiler_params=pltpu.CompilerParams(vmem_limit_bytes=8 * 2**20),
        cost_estimate=pl.CostEstimate(
            flops=60 * cotangent.size, bytes_accessed=16 * cotangent.size, transcendentals=cotangent.size
        ),
        name="activate",
    )(*sums, cotangent)


def reduce4(part, half, shift):
    low, high, every = slice(0, half), slice(half, 2 * half), slice(0, 2 * half)
    leftward = lambda part: lax.ppermute(part.astype(BF16), "col", shift(-1))
    rightward = lambda part: lax.ppermute(part.astype(BF16), "col", shift(1))
    from_right = leftward(cat(part(2, low), part(3, high)))
    from_left = rightward(cat(part(1, low), part(2, high)))
    last_low = leftward(part(3, low) + from_right[low].astype(F32))
    last_high = rightward(part(1, high) + from_left[high].astype(F32))
    return part(0, every), from_left, from_right, last_low, last_high


def total4(own, from_left, from_right, last_low, last_high):
    half = last_low.shape[0]
    near = cat(from_left[:half], from_right[half:]).astype(F32)
    return own + near + cat(last_low, last_high).astype(F32)


def gather4(block, half, shift):
    leftward = lambda part: lax.ppermute(part, "col", shift(-1))
    rightward = lambda part: lax.ppermute(part, "col", shift(1))
    from_right, from_left = leftward(block), rightward(block)
    return block, from_right, leftward(from_right[:half]), rightward(from_left[half:]), from_left


def gather_halves(low, high, shift):
    leftward = lambda part: lax.ppermute(part, "col", shift(-1))
    rightward = lambda part: lax.ppermute(part, "col", shift(1))
    low_right, low_left = leftward(low), rightward(low)
    far_low = leftward(low_right)
    high_left, high_right = rightward(high), leftward(high)
    far_high = rightward(high_left)
    return low, high, low_right, high_right, far_low, far_high, low_left, high_left


def place_grads(blocks, rows, transposed):
    def kernel(*refs):
        target = refs[8]
        col = lax.axis_index("col")
        first, second = (col % 4, col // 4) if transposed else (col // 4, col % 4)
        for n in range(8):
            for i in range(2):
                place = (first + n // 2) % 4, (second + n % 2 * 2 + i) % 4
                target[place] = refs[n][pl.ds(i * rows, rows), :]

    width = blocks[0].shape[1]
    return pl.pallas_call(
        kernel,
        out_shape=jax.ShapeDtypeStruct((4, 4, rows, width), BF16),
        in_specs=[pl.BlockSpec(memory_space=pltpu.VMEM)] * 8,
        out_specs=pl.BlockSpec(memory_space=pltpu.VMEM),
        compiler_params=pltpu.CompilerParams(vmem_limit_bytes=4 * 2**20),
        cost_estimate=pl.CostEstimate(flops=0, bytes_accessed=64 * rows * width, transcendentals=0),
        name="place_grads",
    )(*blocks)


def shards(tokens, weight, cotangent):
    row, col = lax.axis_index("row"), lax.axis_index("col")
    z, core = row // 2, row % 2
    x, y = col // 4, col % 4
    rows = tokens.shape[0] // CHUNKS
    width, hidden_width = weight.shape

    gathered = gather_tokens(tokens)
    hiddens, grads = [], []
    for u in range(CHUNKS):
        full = gathered[u]
        (a, shift_a), (b, shift_b) = ((x, shift_x), (y, shift_y))[:: 1 if u % 2 == 0 else -1]
        near = [pick(full, (a + k) % 4) for k in range(4)]
        near = [n.reshape(4 * rows, width) for n in near]
        summed = total4(*reduce4(lambda k, s: dot(near[k][s], weight), 2 * rows, shift_a))
        summed = summed.reshape(4, rows, hidden_width)
        terms = [pick(summed, (b + k) % 4) for k in range(4)]
        sums = reduce4(lambda k, s: terms[k][s], rows // 2, shift_b)
        hidden, grad = activate(sums, cotangent[u * rows : (u + 1) * rows])
        hiddens.append(hidden)
        own, right, far_low, far_high, left = gather4(grad, rows // 2, shift_b)
        halves = gather_halves(cat(own, right), cat(far_low, far_high, left), shift_a)
        grads.append(place_grads(halves, rows, u % 2 == 1))

    terms, grad_weight = [], None
    for u in range(CHUNKS):
        if u % 2 == 0:
            parity = grads[u].reshape(8, 2, rows, hidden_width)
        else:
            parity = grads[u].reshape(2, 2, 4, rows, hidden_width)
        mine, other = (
            lax.dynamic_index_in_dim(parity, c, 1, False).reshape(8 * rows, hidden_width)
            for c in (core, 1 - core)
        )
        away = lax.ppermute(dot_t(other, weight).astype(BF16), "row", SWAP)
        away = away.reshape(8, rows, width)
        part = lax.optimization_barrier(dot_t(mine, weight).reshape(8, rows, width))
        terms.append((part, away))

    def term(k):
        there = (z + k) % 8
        places = there, there % 2 * 4 + there // 2
        return [pick(part, p) + pick(away, p).astype(F32) for (part, away), p in zip(terms, places)]

    left = lax.ppermute(term(4)[0].astype(BF16), "row", shift_z(-1))
    right = lax.ppermute(term(4)[1].astype(BF16), "row", shift_z(1))
    for step in range(3):
        first, second = term(5 + step)
        if step == 0:
            left = cat((first + left.astype(F32)).astype(BF16), second.astype(BF16))
        else:
            left = (cat(first, second) + left.astype(F32)).astype(BF16)
        first, second = term(3 - step)
        if step == 0:
            right = cat(first.astype(BF16), (second + right.astype(F32)).astype(BF16))
        else:
            right = (cat(first, second) + right.astype(F32)).astype(BF16)
        left = lax.ppermute(left, "row", shift_z(-1))
        right = lax.ppermute(right, "row", shift_z(1))
    grad_tokens = cat(*term(0)) + left.astype(F32) + right.astype(F32)
    for u in range(CHUNKS):
        product = lax.dot_general(
            gathered[u].reshape(-1, width),
            grads[u].reshape(-1, hidden_width),
            (((0,), (0,)), ((), ())),
            preferred_element_type=F32,
        )
        grad_weight = product if grad_weight is None else grad_weight + product
    return cat(*hiddens), grad_weight, grad_tokens.astype(BF16)


def solution(mesh):
    in_specs = (P("row", "col"), P("col", "row"), P("col", "row"))
    out_specs = (P("col", "row"), P("col", "row"), P("row", "col"))
    return jax.shard_map(shards, mesh=mesh, in_specs=in_specs, out_specs=out_specs, check_vma=False)
```
